32 devices in a mesh: rg: 4 (over y, core), az: 8 (over z, x).
Axes of the slice: x: 2, y: 2, z: 4, core: 2. Of those that a mesh axis runs over, the one named last changes fastest.
Arguments:
- raw_pulses: bfloat16 [2, 2048, 65536], P(None, ('rg', 'az')), may hold values from -6 to 6
- range_phase: float32 [65536], replicated, may hold values from -3.140625 to 3.140625
- azimuth_rate: float32 [65536], P(('rg', 'az')), may hold values from 40 to 400
- conc_azimuth: float32 [2048], replicated, may hold values from 0.2 to 1
- conc_range: float32 [65536], replicated, may hold values from 0.2 to 1
Outputs:
- edge_azimuth: float32 [2048, 65536], P(None, ('rg', 'az'))
- edge_range: float32 [2048, 65536], P(('rg', 'az'))
The draws below stay inside these ranges and needn't reach their ends.
All inputs are finite; a program needn't handle non-finite values.
Results may differ from the reference program's by a relative error of at most 0.028.
Values may be sent and summed in bfloat16 or wider, within the bound.
A program may use at most 192 MiB of HBM per device.

```python
import math
import jax
import jax.numpy as jnp
from jax import lax

RA = 256
RB = 256
QA = 32
QB = 64
BINS = 65536
PULSES = 2048


def level_of(key, dims, split, least, top_value):
    def one(axis_at, blocks):
        draws = jax.random.uniform(jax.random.fold_in(jax.random.fold_in(key, 6), axis_at), (blocks,), jnp.float32, least / len(split), top_value / len(split))
        return jnp.repeat(jnp.exp(draws), dims[axis_at] // blocks).reshape((-1,) + (1,) * (len(dims) - axis_at - 1))

    gain = one(*split[0])
    for cut in split[1:]:
        gain = gain * one(*cut)
    return gain


def bell_draw(rng, dims, spread, bound, shards=(), held_as=jnp.bfloat16):
    array = spread * jax.random.normal(rng, dims, jnp.float32)
    if shards:
        array = array * level_of(rng, dims, shards, -0.22, 0.18)
    return jnp.clip(array, -bound, bound).astype(held_as)


def setup_inputs(seed: int = 0) -> dict:
    streams_of = jax.random.split(jax.random.key(seed), 6)
    return {
        "raw_pulses": bell_draw(streams_of[0], (2, PULSES, BINS), 1.0, 6.0, ((1, 32),)),
        "range_phase": jnp.clip(jax.random.uniform(streams_of[1], (BINS,), jnp.float32, -3.140625, 3.140625), -3.140625, 3.140625),
        "azimuth_rate": jnp.clip(jnp.exp(math.log(400.0) - 2.3025851 * jax.random.uniform(streams_of[2], (BINS,), jnp.float32) ** level_of(streams_of[2], (BINS,), ((0, 32),), -0.2, 0.2)), 40.0, 400.0),
        "conc_azimuth": jnp.clip(jax.random.uniform(streams_of[3], (PULSES,), jnp.float32, 0.2, 1.0), 0.2, 1.0),
        "conc_range": jnp.clip(jax.random.uniform(streams_of[4], (BINS,), jnp.float32, 0.2, 1.0), 0.2, 1.0),
    }


def dft_table(length, sign):
    indices = jnp.arange(length, dtype=jnp.int32)
    product = indices[:, None] * indices[None, :] % length
    angles = sign * 2.0 * math.pi / length * product.astype(jnp.float32)
    factor = 1.0 / math.sqrt(length)
    return ((jnp.cos(angles) * factor).astype(jnp.bfloat16), (jnp.sin(angles) * factor).astype(jnp.bfloat16))

def twiddle(first_len, second, sign):
    length_all = first_len * second
    product = jnp.arange(first_len, dtype=jnp.int32)[:, None] * jnp.arange(second, dtype=jnp.int32)[None, :] % length_all
    angles = sign * 2.0 * math.pi / length_all * product.astype(jnp.float32)
    return (jnp.cos(angles), jnp.sin(angles))

def signed_freq(first_len, second):
    length_all = first_len * second
    freqs = jnp.arange(first_len, dtype=jnp.int32)[:, None] + first_len * jnp.arange(second, dtype=jnp.int32)[None, :]
    return jnp.where(freqs < length_all // 2, freqs, freqs - length_all)

def contract(form, matrix, pieces):
    mat_real = matrix[0].astype(jnp.float32)
    mat_imag = matrix[1].astype(jnp.float32)
    if len(pieces) == 1:
        single = pieces[0].astype(jnp.float32)
        return (jnp.einsum(form, mat_real, single), jnp.einsum(form, mat_imag, single))
    real_part = pieces[0].astype(jnp.float32)
    imag_part = pieces[1].astype(jnp.float32)
    return (jnp.einsum(form, mat_real, real_part) - jnp.einsum(form, mat_imag, imag_part), jnp.einsum(form, mat_real, imag_part) + jnp.einsum(form, mat_imag, real_part))

def rotate(pieces, cosine, sine_part):
    return (pieces[0] * cosine - pieces[1] * sine_part, pieces[0] * sine_part + pieces[1] * cosine)

def to_half(pieces):
    return tuple((piece.astype(jnp.bfloat16) for piece in pieces))

def forward(pieces, first_len, second, forms, expand):
    sectioned = contract(forms[0], dft_table(first_len, -1.0), pieces)
    cosine, sine_part = twiddle(first_len, second, -1.0)
    sectioned = to_half(rotate(sectioned, expand(cosine), expand(sine_part)))
    return contract(forms[1], dft_table(second, -1.0), sectioned)

def inverse(pieces, first_len, second, forms, expand, real_only):
    sectioned = contract(forms[2], dft_table(second, 1.0), pieces)
    cosine, sine_part = twiddle(first_len, second, 1.0)
    sectioned = to_half(rotate(sectioned, expand(cosine), expand(sine_part)))
    if real_only:
        mat_real, mat_imag = dft_table(first_len, 1.0)
        return jnp.einsum(forms[3], mat_real.astype(jnp.float32), sectioned[0].astype(jnp.float32)) - jnp.einsum(forms[3], mat_imag.astype(jnp.float32), sectioned[1].astype(jnp.float32))
    return contract(forms[3], dft_table(first_len, 1.0), sectioned)

def range_forms():
    return ('kn,pnb->pkb', 'bm,pkb->pkm', 'mb,pkm->pkb', 'nk,pkb->pnb')

def azimuth_forms():
    return ('ka,abr->kbr', 'bm,kbr->kmr', 'mb,kmr->kbr', 'nk,kbr->nbr')

def range_expand(table):
    return table[None]

def azimuth_expand(table):
    return table[:, :, None]

def concentrate(values, first_len, second, factors, forms, expand):
    spectrum = forward((values,), first_len, second, forms, expand)
    signs = jnp.sign(signed_freq(first_len, second)).astype(jnp.float32)
    weights = expand(signs * factors.reshape(second, first_len).T)
    jumped = to_half((-weights * spectrum[1], weights * spectrum[0]))
    return inverse(jumped, first_len, second, forms, expand, True)

def range_compress(pieces, range_phase):
    count = pieces[0].shape[0]
    shaped = tuple((piece.reshape(count, RA, RB) for piece in pieces))
    spectrum = forward(shaped, RA, RB, range_forms(), range_expand)
    grid = range_phase.reshape(RB, RA).T
    spectrum = to_half(rotate(spectrum, jnp.cos(grid)[None], jnp.sin(grid)[None]))
    result = inverse(spectrum, RA, RB, range_forms(), range_expand, False)
    return tuple((piece.astype(jnp.bfloat16).reshape(count, RA * RB) for piece in result))

def azimuth_part(pieces, rates, conc_azimuth):
    width = pieces[0].shape[1]
    shaped = tuple((piece.reshape(QA, QB, width) for piece in pieces))
    spectrum = forward(shaped, QA, QB, azimuth_forms(), azimuth_expand)
    signed = signed_freq(QA, QB).astype(jnp.float32) / (QA * QB)
    phases = rates[None, None, :] * (signed * signed)[:, :, None]
    spectrum = to_half(rotate(spectrum, jnp.cos(phases), jnp.sin(phases)))
    picture = inverse(spectrum, QA, QB, azimuth_forms(), azimuth_expand, False)
    magnitude = jnp.sqrt(picture[0] * picture[0] + picture[1] * picture[1]).astype(jnp.bfloat16)
    edges = concentrate(magnitude, QA, QB, conc_azimuth, azimuth_forms(), azimuth_expand)
    return (edges.reshape(QA * QB, width), magnitude.reshape(QA * QB, width))

def range_concentrate(rows, conc_range):
    count = rows.shape[0]
    edges = concentrate(rows.reshape(count, RA, RB), RA, RB, conc_range, range_forms(), range_expand)
    return edges.reshape(count, RA * RB)

def reference(raw_pulses, range_phase, azimuth_rate, conc_azimuth, conc_range):
    block_size = 64
    block_count = PULSES // block_size
    blocks = raw_pulses.reshape(2, block_count, block_size, BINS).transpose(1, 0, 2, 3)

    def per_block(block):
        return jnp.stack(range_compress((block[0], block[1]), range_phase))
    compressed = lax.map(per_block, blocks).transpose(1, 0, 2, 3).reshape(2, PULSES, BINS)
    bin_block = min(512, BINS)
    bin_count = BINS // bin_block
    columns = compressed.reshape(2, PULSES, bin_count, bin_block).transpose(2, 0, 1, 3)
    rate_blocks = azimuth_rate.reshape(bin_count, bin_block)

    def per_column(operands):
        column, rates = operands
        return azimuth_part((column[0], column[1]), rates, conc_azimuth)
    edges, magnitudes = lax.map(per_column, (columns, rate_blocks))
    edge_azimuth = edges.transpose(1, 0, 2).reshape(PULSES, BINS)
    magnitude = magnitudes.transpose(1, 0, 2).reshape(PULSES, BINS)
    row_blocks = magnitude.reshape(block_count, block_size, BINS)

    def per_rows(rows):
        return range_concentrate(rows, conc_range)
    edge_range = lax.map(per_rows, row_blocks).reshape(PULSES, BINS)
    return (edge_azimuth, edge_range)
```

```python
import functools
import math

import jax
import jax.numpy as jnp
import numpy as np
from jax import lax
from jax.experimental import pallas as pl
from jax.experimental.pallas import tpu as pltpu
from jax.sharding import PartitionSpec as P

RA = 256
RB = 256
MA = 8
MB = 256
ROWS = 16
CHUNK = 256
LANES = 128
MESH = pl.DeviceIdType.MESH
F32 = jnp.float32
BF16 = jnp.bfloat16
VMEM_LIMIT = 60 * 1024 * 1024


def dft(length, sign):
    grid = np.outer(np.arange(length), np.arange(length)) % length
    angles = sign * 2.0 * np.pi / length * grid
    return np.cos(angles) / math.sqrt(length), np.sin(angles) / math.sqrt(length)


def left_table(length, sign):
    real, imag = dft(length, sign)
    return jnp.asarray(np.block([[real, -imag], [imag, real]]).astype(np.float32), BF16)


def right_table(length, sign):
    real, imag = dft(length, sign)
    return jnp.asarray(np.block([[real, imag], [-imag, real]]).astype(np.float32), BF16)


def twiddle(first, second, sign, scale=1.0):
    grid = np.outer(np.arange(first), np.arange(second)) % (first * second)
    angles = sign * 2.0 * np.pi / (first * second) * grid
    return np.stack([np.cos(angles) * scale, np.sin(angles) * scale]).astype(np.float32)


def dot(a, b):
    return jnp.dot(a, b, preferred_element_type=F32)


def rotated(re, im, cosine, sine):
    return re * cosine - im * sine, re * sine + im * cosine


def pair(re, im, axis):
    return jnp.concatenate([re.astype(BF16), im.astype(BF16)], axis=axis)


def flat_index(naz):
    return lax.axis_index("rg") * naz + lax.axis_index("az")


def coords(flat, naz):
    return (flat // naz, lax.rem(flat, naz))


def greet_all(me, total, naz):
    barrier = pltpu.get_barrier_semaphore()

    def signal(k, carry):
        pl.semaphore_signal(
            barrier, inc=1, device_id=coords(lax.rem(me + k, total), naz), device_id_type=MESH
        )
        return carry

    lax.fori_loop(1, total, signal, 0)
    pl.semaphore_wait(barrier, total - 1)


def range_chain(re, im, fl, fr, gr, gl, wf, wb, middle):
    spec = dot(fl[...], pair(re, im, 0))
    re, im = rotated(spec[:RA], spec[RA:], wf[0], wf[1])
    spec = dot(pair(re, im, 1), fr[...])
    re, im = middle(spec[:, :RB], spec[:, RB:])
    spec = dot(pair(re, im, 1), gr[...])
    re, im = rotated(spec[:, :RB], spec[:, RB:], wb[0], wb[1])
    spec = dot(gl[...], pair(re, im, 0))
    return spec[:RA], spec[RA:]


def compress_kernel(
    total, naz, batches, width, groups,
    raw, phase, fl, fr, gr, gl, wf, wb, rate, afl, agl, awf, awb, squares, turned, mag,
    block, work, ready, x, y, size, load_sem, own_sem, send_sem, recv_sem, x_sem, size_sem,
):
    me = flat_index(naz)
    mine = batches * ROWS
    wide = width // groups

    def load(b, slot):
        return pltpu.make_async_copy(
            raw.at[:, pl.ds(b * ROWS, ROWS), :], block.at[slot], load_sem.at[slot]
        )

    load(0, 0).start()
    greet_all(me, total, naz)

    def send(g, k, start, count):
        peer = lax.rem(me + k, total)
        return pltpu.make_async_remote_copy(
            src_ref=ready.at[:, pl.ds(start, count), pl.ds(peer * width + g * wide, wide)],
            dst_ref=turned.at[:, pl.ds(me * mine + start, count), pl.ds(g * wide, wide)],
            send_sem=send_sem.at[g, k],
            recv_sem=recv_sem.at[g, k],
            device_id=coords(peer, naz),
            device_id_type=MESH,
        )

    def start_group(g, start, count):
        def each(k, carry):
            send(g, k, start, count).start()
            return carry

        lax.fori_loop(1, total, each, 0)

    def own(b):
        return pltpu.make_async_copy(
            ready.at[:, pl.ds(b * ROWS, ROWS), pl.ds(me * width, width)],
            turned.at[:, pl.ds(me * mine + b * ROWS, ROWS), :],
            own_sem.at[b],
        )

    def middle(re, im):
        return rotated(re, im, phase[0], phase[1])

    for b in range(batches):
        slot = b % 2
        if b + 1 < batches:
            load(b + 1, 1 - slot).start()
        load(b, slot).wait()

        def spread(n1, carry):
            for c in range(2):
                piece = block[slot, c, :, pl.ds(pl.multiple_of(n1 * RB, RB), RB)].astype(F32)
                for h in range(2):
                    work[c, h, pl.ds(n1, ROWS, stride=RA), :] = piece[:, h * LANES:(h + 1) * LANES]
            return carry

        lax.fori_loop(0, RA, spread, 0, unroll=4)

        def one_pulse(p, carry):
            rows = pl.ds(pl.multiple_of(p * RA, RA), RA)
            re = jnp.concatenate([work[0, 0, rows, :], work[0, 1, rows, :]], axis=1)
            im = jnp.concatenate([work[1, 0, rows, :], work[1, 1, rows, :]], axis=1)
            res = range_chain(re, im, fl, fr, gr, gl, wf, wb, middle)
            for c in range(2):
                for h in range(2):
                    work[c, h, rows, :] = res[c][:, h * LANES:(h + 1) * LANES]
            return carry

        lax.fori_loop(0, ROWS, one_pulse, 0)

        def gather(n1, carry):
            for c in range(2):
                piece = jnp.concatenate(
                    [work[c, h, pl.ds(n1, ROWS, stride=RA), :] for h in range(2)], axis=1
                )
                ready[c, pl.ds(b * ROWS, ROWS), pl.ds(pl.multiple_of(n1 * RB, RB), RB)] = (
                    piece.astype(BF16)
                )
            return carry

        lax.fori_loop(0, RA, gather, 0, unroll=4)
        start_group(0, b * ROWS, ROWS)
        own(b).start()

    if groups > 1:
        start_group(1, 0, mine)
    for b in range(batches):
        own(b).wait()

    parts = wide // CHUNK

    def column_in(j, slot):
        return pltpu.make_async_copy(
            turned.at[:, :, pl.ds(j * CHUNK, CHUNK)], x.at[slot], x_sem.at[slot]
        )

    def size_out(j):
        return pltpu.make_async_copy(size, mag.at[:, pl.ds(j * CHUNK, CHUNK)], size_sem)

    for g in range(groups):
        def arrive(k, carry):
            send(g, k, 0, mine).wait_recv()
            return carry

        lax.fori_loop(1, total, arrive, 0)
        column_in(g * parts, 0).start()
        if g + 2 < groups:
            start_group(g + 2, 0, mine)
        for part in range(parts):
            j = g * parts + part
            slot = part % 2
            column_in(j, slot).wait()
            if part + 1 < parts:
                column_in(j + 1, 1 - slot).start()
            azimuth_forward(x.at[slot], awf, y)
            azimuth_middle(rate[:, j * CHUNK:(j + 1) * CHUNK], afl, agl, awb, squares, y, work)
            if j > 0:
                size_out(j - 1).wait()
            azimuth_backward(work, size)
            size_out(j).start()
    size_out(groups * parts - 1).wait()

    for g in range(groups):
        def sent(k, carry):
            send(g, k, 0, mine).wait_send()
            return carry

        lax.fori_loop(1, total, sent, 0)


def butterflies(values, sign):
    if len(values) == 1:
        return values
    half = len(values) // 2
    even = butterflies(values[0::2], sign)
    odd = butterflies(values[1::2], sign)
    first, second = [], []
    for k in range(half):
        re, im = odd[k]
        turn = sign * 2.0 * math.pi * k / len(values)
        cosine, sine = math.cos(turn), math.sin(turn)
        if k == 0:
            pass
        elif 4 * k == len(values):
            re, im = (im, -re) if sign < 0 else (-im, re)
        elif abs(abs(cosine) - abs(sine)) < 1e-9:
            size = abs(cosine)
            a = re if cosine > 0 else -re
            b = im if cosine > 0 else -im
            c = re if sine > 0 else -re
            d = im if sine > 0 else -im
            re, im = (a - d) * size, (c + b) * size
        else:
            re, im = re * cosine - im * sine, re * sine + im * cosine
        first.append((even[k][0] + re, even[k][1] + im))
        second.append((even[k][0] - re, even[k][1] - im))
    return first + second


def sincos_fit():
    grid = np.cos(np.linspace(0.0, np.pi, 4001)) * 0.5
    square = grid * grid
    cosine = np.polynomial.chebyshev.Chebyshev.fit(
        square, np.cos(2 * np.pi * grid), 6, domain=[0, 0.25]
    ).convert(kind=np.polynomial.Polynomial).coef
    ratio = np.where(np.abs(grid) < 1e-9, 2 * np.pi, np.sin(2 * np.pi * grid) / np.where(np.abs(grid) < 1e-9, 1.0, grid))
    sine = np.polynomial.chebyshev.Chebyshev.fit(
        square, ratio, 6, domain=[0, 0.25]
    ).convert(kind=np.polynomial.Polynomial).coef
    return [float(x) for x in cosine], [float(x) for x in sine]


def horner(coefs, x):
    value = coefs[-1] * x + coefs[-2]
    for c in coefs[-3::-1]:
        value = value * x + c
    return value


def tile_at(i):
    t, h = i // 2, lax.rem(i, 2)
    return t * ROWS, pl.ds(pl.multiple_of(h * LANES, LANES), LANES)


def rows_at(start):
    return pl.ds(pl.multiple_of(start, ROWS), ROWS)


def azimuth_forward(x, wf, y):
    def one(i, carry):
        top, lanes = tile_at(i)
        values = [
            tuple(x[c, rows_at(m * MB + top), lanes].astype(F32) for c in range(2))
            for m in range(MA)
        ]
        for f, (re, im) in enumerate(butterflies(values, -1.0)):
            re, im = rotated(re, im, wf[0, f, rows_at(top), :], wf[1, f, rows_at(top), :])
            y[f, rows_at(top), lanes] = re.astype(BF16)
            y[f, rows_at(MB + top), lanes] = im.astype(BF16)
        return carry

    lax.fori_loop(0, 2 * (MB // ROWS), one, 0)


def azimuth_middle(rate, fl, gl, wb, squares, y, z):
    cos_fit, sin_fit = sincos_fit()
    turns = rate * (1.0 / (2.0 * math.pi))

    def one(f, carry):
        spec = dot(fl[...], y[f])
        square = jnp.concatenate([squares[f], squares[f]], axis=1)
        turn = turns * square
        turn = turn - jnp.round(turn)
        power = turn * turn
        re, im = rotated(spec[:MB], spec[MB:], horner(cos_fit, power), horner(sin_fit, power) * turn)
        spec = dot(gl[...], pair(re, im, 0))
        cosine = jnp.concatenate([wb[0, f], wb[0, f]], axis=1)
        sine = jnp.concatenate([wb[1, f], wb[1, f]], axis=1)
        rows = pl.ds(pl.multiple_of(f * MB, MB), MB)
        for c, piece in enumerate(rotated(spec[:MB], spec[MB:], cosine, sine)):
            for h in range(2):
                z[c, h, rows, :] = piece[:, h * LANES:(h + 1) * LANES]
        return carry

    lax.fori_loop(0, MA, one, 0)


def azimuth_backward(z, size):
    for h in range(2):
        def one(t, carry):
            top = t * ROWS
            values = [
                tuple(z[c, h, rows_at(f * MB + top), :] for c in range(2)) for f in range(MA)
            ]
            for m, (re, im) in enumerate(butterflies(values, 1.0)):
                size[rows_at(m * MB + top), h * LANES:(h + 1) * LANES] = (
                    jnp.sqrt(re * re + im * im).astype(BF16)
                )
            return carry

        lax.fori_loop(0, MB // ROWS, one, 0)


def edge_kernel(
    total, naz, batches, width,
    mag, kernel_row, weights, fl, fr, gr, gl, wf, wb, edge_az, edge_rg,
    rows_in, work, rows_out, matrix, column, column_out,
    own_sem, column_sem, column_out_sem, rows_sem, send_sem, recv_sem,
):
    me = flat_index(naz)
    mine = batches * ROWS
    greet_all(me, total, naz)

    def send(b, k):
        peer = lax.rem(me + k, total)
        return pltpu.make_async_remote_copy(
            src_ref=mag.at[pl.ds(peer * mine + b * ROWS, ROWS), :],
            dst_ref=rows_in.at[pl.ds(b * ROWS, ROWS), pl.ds(me * width, width)],
            send_sem=send_sem.at[b, k],
            recv_sem=recv_sem.at[b, k],
            device_id=coords(peer, naz),
            device_id_type=MESH,
        )

    def own(b):
        return pltpu.make_async_copy(
            mag.at[pl.ds(me * mine + b * ROWS, ROWS), :],
            rows_in.at[pl.ds(b * ROWS, ROWS), pl.ds(me * width, width)],
            own_sem.at[b],
        )

    def start_batch(b, carry):
        def start(k, inner):
            send(b, k).start()
            return inner

        lax.fori_loop(1, total, start, 0)
        own(b).start()
        return carry

    lax.fori_loop(0, batches, start_batch, 0)

    pulses = MA * MB
    base = jnp.broadcast_to(kernel_row[...], (MB, pulses))
    base = pltpu.roll(base, 0, 1, stride=1, stride_axis=0).astype(BF16)
    for m in range(MA):
        cut = pulses - m * MB
        rolled = base if m == 0 else jnp.concatenate([base[:, cut:], base[:, :cut]], axis=1)
        matrix[m * MB:(m + 1) * MB, :] = rolled

    chunks = width // CHUNK

    def column_in(j, slot):
        return pltpu.make_async_copy(
            mag.at[:, pl.ds(j * CHUNK, CHUNK)], column.at[slot], column_sem.at[slot]
        )

    def column_back(j, slot):
        return pltpu.make_async_copy(
            column_out.at[slot], edge_az.at[:, pl.ds(j * CHUNK, CHUNK)], column_out_sem.at[slot]
        )

    column_in(0, 0).start()
    for j in range(chunks):
        slot = j % 2
        if j + 1 < chunks:
            column_in(j + 1, 1 - slot).start()
        column_in(j, slot).wait()
        if j >= 2:
            column_back(j - 2, slot).wait()

        def part(m, carry):
            rows = pl.ds(pl.multiple_of(m * MB, MB), MB)
            column_out[slot, rows, :] = dot(matrix[rows, :], column[slot])
            return carry

        lax.fori_loop(0, MA, part, 0)
        column_back(j, slot).start()
    for j in range(max(chunks - 2, 0), chunks):
        column_back(j, j % 2).wait()

    def middle(re, im):
        return -weights[...] * im, weights[...] * re

    def rows_back(b, slot):
        return pltpu.make_async_copy(
            rows_out.at[slot], edge_rg.at[pl.ds(b * ROWS, ROWS), :], rows_sem.at[slot]
        )

    for b in range(batches):
        slot = b % 2

        def arrive(k, carry):
            send(b, k).wait_recv()
            return carry

        lax.fori_loop(1, total, arrive, 0)
        own(b).wait()

        def spread(n1, carry):
            piece = rows_in[pl.ds(b * ROWS, ROWS), pl.ds(pl.multiple_of(n1 * RB, RB), RB)].astype(F32)
            for h in range(2):
                work[h, pl.ds(n1, ROWS, stride=RA), :] = piece[:, h * LANES:(h + 1) * LANES]
            return carry

        lax.fori_loop(0, RA, spread, 0, unroll=4)

        def one_pair(q, carry):
            both = [pl.ds(pl.multiple_of((q + o) * RA, RA), RA) for o in (0, ROWS // 2)]
            re, im = (jnp.concatenate([work[0, r, :], work[1, r, :]], axis=1) for r in both)
            res = range_chain(re, im, fl, fr, gr, gl, wf, wb, middle)
            for c in range(2):
                for h in range(2):
                    work[h, both[c], :] = res[c][:, h * LANES:(h + 1) * LANES]
            return carry

        lax.fori_loop(0, ROWS // 2, one_pair, 0)
        if b >= 2:
            rows_back(b - 2, slot).wait()

        def gather(n1, carry):
            piece = jnp.concatenate([work[h, pl.ds(n1, ROWS, stride=RA), :] for h in range(2)], axis=1)
            rows_out[slot, :, pl.ds(pl.multiple_of(n1 * RB, RB), RB)] = piece
            return carry

        lax.fori_loop(0, RA, gather, 0, unroll=4)
        rows_back(b, slot).start()
    for b in range(max(batches - 2, 0), batches):
        rows_back(b, b % 2).wait()

    def sent(b, carry):
        def each(k, inner):
            send(b, k).wait_send()
            return inner

        return lax.fori_loop(1, total, each, carry)

    lax.fori_loop(0, batches, sent, 0)


def lane_table(table):
    return jnp.broadcast_to(jnp.asarray(table)[..., None], table.shape + (LANES,))


def on_device(total, naz, raw_pulses, range_phase, azimuth_rate, conc_azimuth, conc_range):
    mine, bins = raw_pulses.shape[1], raw_pulses.shape[2]
    width = azimuth_rate.shape[0]
    pulses = conc_azimuth.shape[0]
    batches = mine // ROWS
    vmem = pl.BlockSpec(memory_space=pltpu.VMEM)
    hbm = pl.BlockSpec(memory_space=pl.ANY)
    range_tables = (left_table(RA, -1.0), right_table(RB, -1.0), right_table(RB, 1.0), left_table(RA, 1.0))
    range_twiddles = (jnp.asarray(twiddle(RA, RB, -1.0)), jnp.asarray(twiddle(RA, RB, 1.0)))

    with jax.named_scope("compress"):
        groups = max(1, min(4, width // CHUNK))
        grid = range_phase.reshape(RB, RA).T
        phase = jnp.stack([jnp.cos(grid), jnp.sin(grid)])
        scale = 1.0 / math.sqrt(MA)
        freqs = np.arange(MA)[:, None] + MA * np.arange(MB)[None, :]
        signed = np.where(freqs < pulses // 2, freqs, freqs - pulses) / pulses
        squares = lane_table((signed * signed).astype(np.float32))
        _, magnitude = pl.pallas_call(
            functools.partial(compress_kernel, total, naz, batches, width, groups),
            out_shape=(
                jax.ShapeDtypeStruct((2, pulses, width), BF16),
                jax.ShapeDtypeStruct((pulses, width), BF16),
            ),
            in_specs=[hbm] + [vmem] * 13,
            out_specs=(hbm, hbm),
            scratch_shapes=[
                pltpu.VMEM((2, 2, ROWS, bins), BF16),
                pltpu.VMEM((2, 2, ROWS * RA, LANES), F32),
                pltpu.VMEM((2, mine, bins), BF16),
                pltpu.VMEM((2, 2, pulses, CHUNK), BF16),
                pltpu.VMEM((MA, 2 * MB, CHUNK), BF16),
                pltpu.VMEM((pulses, CHUNK), BF16),
                pltpu.SemaphoreType.DMA((2,)),
                pltpu.SemaphoreType.DMA((batches,)),
                pltpu.SemaphoreType.DMA((groups, total)),
                pltpu.SemaphoreType.DMA((groups, total)),
                pltpu.SemaphoreType.DMA((2,)),
                pltpu.SemaphoreType.DMA,
            ],
            compiler_params=pltpu.CompilerParams(
                collective_id=0, has_side_effects=True, vmem_limit_bytes=VMEM_LIMIT
            ),
            name="compress",
        )(
            raw_pulses, phase, *range_tables, *range_twiddles,
            azimuth_rate.reshape(1, width), left_table(MB, -1.0), left_table(MB, 1.0),
            lane_table(twiddle(MA, MB, -1.0, scale)), lane_table(twiddle(MA, MB, 1.0, scale)), squares,
        )

    with jax.named_scope("edge_maps"):
        half = pulses // 2
        mixed = conc_azimuth[1:half] + conc_azimuth[:half:-1]
        index = np.arange(1, half)
        sines = np.sin(2.0 * np.pi / pulses * (np.outer(index, index) % pulses)) / pulses
        taps = jnp.sum(jnp.asarray(sines.astype(np.float32)) * mixed[None, :], axis=1)
        zero = jnp.zeros((1,), F32)
        kernel_row = jnp.concatenate([zero, taps, zero, -taps[::-1]]).reshape(1, pulses)
        mirrored = jnp.concatenate([conc_range[:1], conc_range[:0:-1]])
        place = jnp.arange(bins, dtype=jnp.int32)
        signs = jnp.where(place < bins // 2, 1.0, -1.0) * ((place != 0) & (place != bins // 2))
        weights = (0.5 * signs * (conc_range + mirrored)).reshape(RB, RA).T
        return pl.pallas_call(
            functools.partial(edge_kernel, total, naz, batches, width),
            out_shape=(
                jax.ShapeDtypeStruct((pulses, width), F32),
                jax.ShapeDtypeStruct((mine, bins), F32),
            ),
            in_specs=[hbm] + [vmem] * 8,
            out_specs=(hbm, hbm),
            scratch_shapes=[
                pltpu.VMEM((mine, bins), BF16),
                pltpu.VMEM((2, ROWS * RA, LANES), F32),
                pltpu.VMEM((2, ROWS, bins), F32),
                pltpu.VMEM((pulses, pulses), BF16),
                pltpu.VMEM((2, pulses, CHUNK), BF16),
                pltpu.VMEM((2, pulses, CHUNK), F32),
                pltpu.SemaphoreType.DMA((batches,)),
                pltpu.SemaphoreType.DMA((2,)),
                pltpu.SemaphoreType.DMA((2,)),
                pltpu.SemaphoreType.DMA((2,)),
                pltpu.SemaphoreType.DMA((batches, total)),
                pltpu.SemaphoreType.DMA((batches, total)),
            ],
            compiler_params=pltpu.CompilerParams(
                collective_id=1, has_side_effects=True, vmem_limit_bytes=VMEM_LIMIT
            ),
            name="edge_maps",
        )(magnitude, kernel_row, weights, *range_tables, *range_twiddles)


def solution(mesh):
    total = mesh.shape["rg"] * mesh.shape["az"]
    in_specs = (P(None, ("rg", "az"), None), P(), P(("rg", "az")), P(), P())
    out_specs = (P(None, ("rg", "az")), P(("rg", "az"), None))
    return jax.shard_map(
        functools.partial(on_device, total, mesh.shape["az"]),
        mesh=mesh, in_specs=in_specs, out_specs=out_specs, check_vma=False,
    )
```

```python
import functools
import math

import jax
import jax.numpy as jnp
import numpy as np
from jax import lax
from jax.experimental import pallas as pl
from jax.experimental.pallas import tpu as pltpu
from jax.sharding import PartitionSpec as P

RA = 256
RB = 256
MA = 8
MB = 256
ROWS = 16
CHUNK = 256
LANES = 128
MESH = pl.DeviceIdType.MESH
F32 = jnp.float32
BF16 = jnp.bfloat16
VMEM_LIMIT = 60 * 1024 * 1024


def dft(length, sign):
    grid = np.outer(np.arange(length), np.arange(length)) % length
    angles = sign * 2.0 * np.pi / length * grid
    return np.cos(angles) / math.sqrt(length), np.sin(angles) / math.sqrt(length)


def left_table(length, sign):
    real, imag = dft(length, sign)
    return jnp.asarray(np.block([[real, -imag], [imag, real]]).astype(np.float32), BF16)


def right_table(length, sign):
    real, imag = dft(length, sign)
    return jnp.asarray(np.block([[real, imag], [-imag, real]]).astype(np.float32), BF16)


def twiddle(first, second, sign, scale=1.0):
    grid = np.outer(np.arange(first), np.arange(second)) % (first * second)
    angles = sign * 2.0 * np.pi / (first * second) * grid
    return np.stack([np.cos(angles) * scale, np.sin(angles) * scale]).astype(np.float32)


def dot(a, b):
    return jnp.dot(a, b, preferred_element_type=F32)


def rotated(re, im, cosine, sine):
    return re * cosine - im * sine, re * sine + im * cosine


def pair(re, im, axis):
    return jnp.concatenate([re.astype(BF16), im.astype(BF16)], axis=axis)


def flat_index(naz):
    return lax.axis_index("rg") * naz + lax.axis_index("az")


def coords(flat, naz):
    return (flat // naz, lax.rem(flat, naz))


def greet_all(me, total, naz):
    barrier = pltpu.get_barrier_semaphore()

    def signal(k, carry):
        pl.semaphore_signal(
            barrier, inc=1, device_id=coords(lax.rem(me + k, total), naz), device_id_type=MESH
        )
        return carry

    lax.fori_loop(1, total, signal, 0)
    pl.semaphore_wait(barrier, total - 1)


def range_chain(re, im, fl, fr, gr, gl, wf, wb, middle):
    spec = dot(fl[...], pair(re, im, 0))
    re, im = rotated(spec[:RA], spec[RA:], wf[0], wf[1])
    spec = dot(pair(re, im, 1), fr[...])
    re, im = middle(spec[:, :RB], spec[:, RB:])
    spec = dot(pair(re, im, 1), gr[...])
    re, im = rotated(spec[:, :RB], spec[:, RB:], wb[0], wb[1])
    spec = dot(gl[...], pair(re, im, 0))
    return spec[:RA], spec[RA:]


def image_kernel(
    total, naz, batches, width, groups,
    raw, phase, fl, fr, gr, gl, wf, wb, rate, awf, awb, squares, kernel_row, weights,
    turned, mag, rows_in, edge_az, edge_rg,
    block, work, ready, x, y, size, base, column_out, rows_out,
    load_sem, own_sem, send_sem, recv_sem, x_sem, size_sem, column_sem, rows_sem,
    early_send, early_recv, late_send, late_recv,
):
    me = flat_index(naz)
    mine = batches * ROWS
    wide = width // groups
    pulses = MA * MB
    eager = min(2, groups)

    def load(b, slot):
        return pltpu.make_async_copy(
            raw.at[:, pl.ds(b * ROWS, ROWS), :], block.at[slot], load_sem.at[slot]
        )

    load(0, 0).start()
    greet_all(me, total, naz)

    def over_peers(act):
        def each(k, carry):
            act(k)
            return carry

        lax.fori_loop(1, total, each, 0)

    def send(g, k, start, count):
        peer = lax.rem(me + k, total)
        return pltpu.make_async_remote_copy(
            src_ref=ready.at[:, pl.ds(start, count), pl.ds(peer * width + g * wide, wide)],
            dst_ref=turned.at[:, pl.ds(me * mine + start, count), pl.ds(g * wide, wide)],
            send_sem=send_sem.at[g, k],
            recv_sem=recv_sem.at[g, k],
            device_id=coords(peer, naz),
            device_id_type=MESH,
        )

    def own(b):
        return pltpu.make_async_copy(
            ready.at[:, pl.ds(b * ROWS, ROWS), pl.ds(me * width, width)],
            turned.at[:, pl.ds(me * mine + b * ROWS, ROWS), :],
            own_sem.at[b],
        )

    def middle(re, im):
        return rotated(re, im, phase[0], phase[1])

    for b in range(batches):
        slot = b % 2
        if b + 1 < batches:
            load(b + 1, 1 - slot).start()
        load(b, slot).wait()

        def spread(n1, carry):
            for c in range(2):
                piece = block[slot, c, :, pl.ds(pl.multiple_of(n1 * RB, RB), RB)].astype(F32)
                for h in range(2):
                    work[c, h, pl.ds(n1, ROWS, stride=RA), :] = piece[:, h * LANES:(h + 1) * LANES]
            return carry

        lax.fori_loop(0, RA, spread, 0, unroll=4)

        def one_pulse(p, carry):
            rows = pl.ds(pl.multiple_of(p * RA, RA), RA)
            re = jnp.concatenate([work[0, 0, rows, :], work[0, 1, rows, :]], axis=1)
            im = jnp.concatenate([work[1, 0, rows, :], work[1, 1, rows, :]], axis=1)
            res = range_chain(re, im, fl, fr, gr, gl, wf, wb, middle)
            for c in range(2):
                for h in range(2):
                    work[c, h, rows, :] = res[c][:, h * LANES:(h + 1) * LANES]
            return carry

        lax.fori_loop(0, ROWS, one_pulse, 0, unroll=2)

        def gather(n1, carry):
            for c in range(2):
                piece = jnp.concatenate(
                    [work[c, h, pl.ds(n1, ROWS, stride=RA), :] for h in range(2)], axis=1
                )
                ready[c, pl.ds(b * ROWS, ROWS), pl.ds(pl.multiple_of(n1 * RB, RB), RB)] = (
                    piece.astype(BF16)
                )
            return carry

        lax.fori_loop(0, RA, gather, 0, unroll=4)
        for g in range(eager):
            over_peers(lambda k: send(g, k, b * ROWS, ROWS).start())
        own(b).start()

    taps = jnp.broadcast_to(kernel_row[...], (MB, pulses))
    base[...] = pltpu.roll(taps, 0, 1, stride=1, stride_axis=0).astype(BF16)
    for b in range(batches):
        own(b).wait()

    parts = wide // CHUNK
    early = (groups - 1) * wide

    def column_in(j, slot):
        return pltpu.make_async_copy(
            turned.at[:, :, pl.ds(j * CHUNK, CHUNK)], x.at[slot], x_sem.at[slot]
        )

    def size_out(j):
        return pltpu.make_async_copy(
            size.at[pl.ds(0, pulses), :], mag.at[:, pl.ds(j * CHUNK, CHUNK)], size_sem
        )

    def column_back(j):
        return pltpu.make_async_copy(
            column_out, edge_az.at[:, pl.ds(j * CHUNK, CHUNK)], column_sem
        )

    def send_back(k, row, rows, column, columns, sent_sem, here_sem):
        peer = lax.rem(me + k, total)
        return pltpu.make_async_remote_copy(
            src_ref=mag.at[pl.ds(peer * mine + row, rows), pl.ds(column, columns)],
            dst_ref=rows_in.at[pl.ds(row, rows), pl.ds(me * width + column, columns)],
            send_sem=sent_sem,
            recv_sem=here_sem,
            device_id=coords(peer, naz),
            device_id_type=MESH,
        )

    def send_early(k, column, columns):
        return send_back(k, 0, mine, column, columns, early_send.at[k], early_recv.at[k])

    def send_late(k, b):
        return send_back(
            k, b * ROWS, ROWS, early, wide, late_send.at[b, k], late_recv.at[b, k]
        )

    for g in range(groups):
        over_peers(lambda k: send(g, k, 0, mine).wait_recv())
        column_in(g * parts, 0).start()
        if g + eager < groups:
            over_peers(lambda k: send(g + eager, k, 0, mine).start())
        for part in range(parts):
            j = g * parts + part
            slot = part % 2
            column_in(j, slot).wait()
            if part + 1 < parts:
                column_in(j + 1, 1 - slot).start()
            azimuth_forward(x.at[slot], awf, y)
            azimuth_middle(rate[:, j * CHUNK:(j + 1) * CHUNK], fl, gl, awb, squares, y, work)
            azimuth_backward(work, size)
            size_out(j).start()
            if part + 1 == parts:
                size_out(j).wait()
                if g + 1 < groups:
                    over_peers(lambda k: send_early(k, g * wide, wide).start())
                else:
                    for b in range(min(2, batches)):
                        over_peers(lambda k: send_late(k, b).start())
            if j > 0:
                column_back(j - 1).wait()

            def edges(m, carry):
                rows = pl.ds(pl.multiple_of(m * MB, MB), MB)
                column_out[rows, :] = dot(base[...], size[pl.ds(pl.multiple_of(m * MB, MB), pulses), :])
                return carry

            lax.fori_loop(0, MA, edges, 0)
            column_back(j).start()
            if part + 1 < parts:
                size_out(j).wait()
    own_rows = pltpu.make_async_copy(
        mag.at[pl.ds(me * mine, mine), :], rows_in.at[:, pl.ds(me * width, width)], size_sem
    )
    own_rows.start()
    own_rows.wait()
    column_back(groups * parts - 1).wait()
    if early:
        over_peers(lambda k: send_early(k, 0, early).wait_recv())

    def turn(re, im):
        return -weights[...] * im, weights[...] * re

    def rows_load(b):
        return pltpu.make_async_copy(
            rows_in.at[pl.ds(b * ROWS, ROWS), :], block.at[0, 0], load_sem.at[0]
        )

    def rows_back(b):
        return pltpu.make_async_copy(rows_out, edge_rg.at[pl.ds(b * ROWS, ROWS), :], rows_sem)

    for b in range(batches):
        over_peers(lambda k: send_late(k, b).wait_recv())
        if b + 2 < batches:
            over_peers(lambda k: send_late(k, b + 2).start())
        rows_load(b).start()
        rows_load(b).wait()

        def spread_rows(n1, carry):
            piece = block[0, 0, :, pl.ds(pl.multiple_of(n1 * RB, RB), RB)].astype(F32)
            for h in range(2):
                work[0, h, pl.ds(n1, ROWS, stride=RA), :] = piece[:, h * LANES:(h + 1) * LANES]
            return carry

        lax.fori_loop(0, RA, spread_rows, 0, unroll=4)

        def one_pair(q, carry):
            both = [pl.ds(pl.multiple_of((q + o) * RA, RA), RA) for o in (0, ROWS // 2)]
            re, im = (jnp.concatenate([work[0, 0, r, :], work[0, 1, r, :]], axis=1) for r in both)
            res = range_chain(re, im, fl, fr, gr, gl, wf, wb, turn)
            for c in range(2):
                for h in range(2):
                    work[0, h, both[c], :] = res[c][:, h * LANES:(h + 1) * LANES]
            return carry

        lax.fori_loop(0, ROWS // 2, one_pair, 0, unroll=2)
        if b > 0:
            rows_back(b - 1).wait()

        def gather_rows(n1, carry):
            piece = jnp.concatenate(
                [work[0, h, pl.ds(n1, ROWS, stride=RA), :] for h in range(2)], axis=1
            )
            rows_out[:, pl.ds(pl.multiple_of(n1 * RB, RB), RB)] = piece
            return carry

        lax.fori_loop(0, RA, gather_rows, 0, unroll=4)
        rows_back(b).start()
    rows_back(batches - 1).wait()

    for g in range(groups):
        over_peers(lambda k: send(g, k, 0, mine).wait_send())
    if early:
        over_peers(lambda k: send_early(k, 0, early).wait_send())
    for b in range(batches):
        over_peers(lambda k: send_late(k, b).wait_send())


def butterflies(values, sign):
    if len(values) == 1:
        return values
    half = len(values) // 2
    even = butterflies(values[0::2], sign)
    odd = butterflies(values[1::2], sign)
    first, second = [], []
    for k in range(half):
        re, im = odd[k]
        turn = sign * 2.0 * math.pi * k / len(values)
        cosine, sine = math.cos(turn), math.sin(turn)
        if k == 0:
            pass
        elif 4 * k == len(values):
            re, im = (im, -re) if sign < 0 else (-im, re)
        elif abs(abs(cosine) - abs(sine)) < 1e-9:
            size = abs(cosine)
            a = re if cosine > 0 else -re
            b = im if cosine > 0 else -im
            c = re if sine > 0 else -re
            d = im if sine > 0 else -im
            re, im = (a - d) * size, (c + b) * size
        else:
            re, im = re * cosine - im * sine, re * sine + im * cosine
        first.append((even[k][0] + re, even[k][1] + im))
        second.append((even[k][0] - re, even[k][1] - im))
    return first + second


def sincos_fit():
    grid = np.cos(np.linspace(0.0, np.pi, 4001)) * 0.5
    square = grid * grid
    cosine = np.polynomial.chebyshev.Chebyshev.fit(
        square, np.cos(2 * np.pi * grid), 6, domain=[0, 0.25]
    ).convert(kind=np.polynomial.Polynomial).coef
    ratio = np.where(np.abs(grid) < 1e-9, 2 * np.pi, np.sin(2 * np.pi * grid) / np.where(np.abs(grid) < 1e-9, 1.0, grid))
    sine = np.polynomial.chebyshev.Chebyshev.fit(
        square, ratio, 6, domain=[0, 0.25]
    ).convert(kind=np.polynomial.Polynomial).coef
    return [float(x) for x in cosine], [float(x) for x in sine]


def horner(coefs, x):
    value = coefs[-1] * x + coefs[-2]
    for c in coefs[-3::-1]:
        value = value * x + c
    return value


def tile_at(i):
    t, h = i // 2, lax.rem(i, 2)
    return t * ROWS, pl.ds(pl.multiple_of(h * LANES, LANES), LANES)


def rows_at(start):
    return pl.ds(pl.multiple_of(start, ROWS), ROWS)


def azimuth_forward(x, wf, y):
    def one(i, carry):
        top, lanes = tile_at(i)
        values = [
            tuple(x[c, rows_at(m * MB + top), lanes].astype(F32) for c in range(2))
            for m in range(MA)
        ]
        for f, (re, im) in enumerate(butterflies(values, -1.0)):
            re, im = rotated(re, im, wf[0, f, rows_at(top), :], wf[1, f, rows_at(top), :])
            y[f, rows_at(top), lanes] = re.astype(BF16)
            y[f, rows_at(MB + top), lanes] = im.astype(BF16)
        return carry

    lax.fori_loop(0, 2 * (MB // ROWS), one, 0)


def azimuth_middle(rate, fl, gl, wb, squares, y, z):
    cos_fit, sin_fit = sincos_fit()
    turns = rate * (1.0 / (2.0 * math.pi))

    def one(f, carry):
        spec = dot(fl[...], y[f])
        square = jnp.concatenate([squares[f], squares[f]], axis=1)
        turn = turns * square
        turn = turn - jnp.round(turn)
        power = turn * turn
        re, im = rotated(spec[:MB], spec[MB:], horner(cos_fit, power), horner(sin_fit, power) * turn)
        spec = dot(gl[...], pair(re, im, 0))
        cosine = jnp.concatenate([wb[0, f], wb[0, f]], axis=1)
        sine = jnp.concatenate([wb[1, f], wb[1, f]], axis=1)
        rows = pl.ds(pl.multiple_of(f * MB, MB), MB)
        for c, piece in enumerate(rotated(spec[:MB], spec[MB:], cosine, sine)):
            for h in range(2):
                z[c, h, rows, :] = piece[:, h * LANES:(h + 1) * LANES]
        return carry

    lax.fori_loop(0, MA, one, 0)


def azimuth_backward(z, size):
    for h in range(2):
        def one(t, carry):
            top = t * ROWS
            values = [
                tuple(z[c, h, rows_at(f * MB + top), :] for c in range(2)) for f in range(MA)
            ]
            for m, (re, im) in enumerate(butterflies(values, 1.0)):
                value = jnp.sqrt(re * re + im * im).astype(BF16)
                for copy in range(2):
                    rows = rows_at((copy * MA + m) * MB + top)
                    size[rows, h * LANES:(h + 1) * LANES] = value
            return carry

        lax.fori_loop(0, MB // ROWS, one, 0)


def lane_table(table):
    return jnp.asarray(np.repeat(table[..., None], LANES, axis=-1))


def on_device(total, naz, raw_pulses, range_phase, azimuth_rate, conc_azimuth, conc_range):
    mine, bins = raw_pulses.shape[1], raw_pulses.shape[2]
    width = azimuth_rate.shape[0]
    pulses = conc_azimuth.shape[0]
    batches = mine // ROWS
    vmem = pl.BlockSpec(memory_space=pltpu.VMEM)
    hbm = pl.BlockSpec(memory_space=pl.ANY)
    range_tables = (left_table(RA, -1.0), right_table(RB, -1.0), right_table(RB, 1.0), left_table(RA, 1.0))
    range_twiddles = (jnp.asarray(twiddle(RA, RB, -1.0)), jnp.asarray(twiddle(RA, RB, 1.0)))

    with jax.named_scope("tables"):
        groups = max(1, min(4, width // CHUNK))
        grid = range_phase.reshape(RB, RA).T
        phase = jnp.stack([jnp.cos(grid), jnp.sin(grid)])
        scale = 1.0 / math.sqrt(MA)
        freqs = np.arange(MA)[:, None] + MA * np.arange(MB)[None, :]
        signed = np.where(freqs < pulses // 2, freqs, freqs - pulses) / pulses
        squares = lane_table((signed * signed).astype(np.float32))
        half = pulses // 2
        mixed = conc_azimuth[1:half] + conc_azimuth[:half:-1]
        index = np.arange(1, half)
        sines = np.sin(2.0 * np.pi / pulses * (np.outer(index, index) % pulses)) / pulses
        taps = jnp.sum(jnp.asarray(sines.astype(np.float32)) * mixed[None, :], axis=1)
        zero = jnp.zeros((1,), F32)
        kernel_row = jnp.concatenate([zero, taps, zero, -taps[::-1]]).reshape(1, pulses)
        mirrored = jnp.concatenate([conc_range[:1], conc_range[:0:-1]])
        place = jnp.arange(bins, dtype=jnp.int32)
        signs = jnp.where(place < bins // 2, 1.0, -1.0) * ((place != 0) & (place != bins // 2))
        weights = (0.5 * signs * (conc_range + mirrored)).reshape(RB, RA).T

    with jax.named_scope("image"):
        dma = pltpu.SemaphoreType.DMA
        _, _, _, edge_azimuth, edge_range = pl.pallas_call(
            functools.partial(image_kernel, total, naz, batches, width, groups),
            out_shape=(
                jax.ShapeDtypeStruct((2, pulses, width), BF16),
                jax.ShapeDtypeStruct((pulses, width), BF16),
                jax.ShapeDtypeStruct((mine, bins), BF16),
                jax.ShapeDtypeStruct((pulses, width), F32),
                jax.ShapeDtypeStruct((mine, bins), F32),
            ),
            in_specs=[hbm] + [vmem] * 13,
            out_specs=(hbm,) * 5,
            scratch_shapes=[
                pltpu.VMEM((2, 2, ROWS, bins), BF16),
                pltpu.VMEM((2, 2, ROWS * RA, LANES), F32),
                pltpu.VMEM((2, mine, bins), BF16),
                pltpu.VMEM((2, 2, pulses, CHUNK), BF16),
                pltpu.VMEM((MA, 2 * MB, CHUNK), BF16),
                pltpu.VMEM((2 * pulses, CHUNK), BF16),
                pltpu.VMEM((MB, pulses), BF16),
                pltpu.VMEM((pulses, CHUNK), F32),
                pltpu.VMEM((ROWS, bins), F32),
                dma((2,)), dma((batches,)), dma((groups, total)), dma((groups, total)),
                dma((2,)), dma, dma, dma,
                dma((total,)), dma((total,)), dma((batches, total)), dma((batches, total)),
            ],
            compiler_params=pltpu.CompilerParams(
                collective_id=0, has_side_effects=True, vmem_limit_bytes=VMEM_LIMIT
            ),
            name="image",
        )(
            raw_pulses, phase, *range_tables, *range_twiddles, azimuth_rate.reshape(1, width),
            lane_table(twiddle(MA, MB, -1.0, scale)), lane_table(twiddle(MA, MB, 1.0, scale)),
            squares, kernel_row, weights,
        )
    return edge_azimuth, edge_range


def solution(mesh):
    total = mesh.shape["rg"] * mesh.shape["az"]
    in_specs = (P(None, ("rg", "az"), None), P(), P(("rg", "az")), P(), P())
    out_specs = (P(None, ("rg", "az")), P(("rg", "az"), None))
    return jax.shard_map(
        functools.partial(on_device, total, mesh.shape["az"]),
        mesh=mesh, in_specs=in_specs, out_specs=out_specs, check_vma=False,
    )
```

```python
import functools
import math

import jax
import jax.numpy as jnp
import numpy as np
from jax import lax
from jax.experimental import pallas as pl
from jax.experimental.pallas import tpu as pltpu
from jax.sharding import PartitionSpec as P

RA = 256
RB = 256
MA = 8
MB = 256
ROWS = 16
CHUNK = 256
LANES = 128
MESH = pl.DeviceIdType.MESH
F32 = jnp.float32
BF16 = jnp.bfloat16
VMEM_LIMIT = 60 * 1024 * 1024


def dft(length, sign):
    grid = np.outer(np.arange(length), np.arange(length)) % length
    angles = sign * 2.0 * np.pi / length * grid
    return np.cos(angles) / math.sqrt(length), np.sin(angles) / math.sqrt(length)


def left_table(length, sign):
    real, imag = dft(length, sign)
    return jnp.asarray(np.block([[real, -imag], [imag, real]]).astype(np.float32), BF16)


def right_table(length, sign):
    real, imag = dft(length, sign)
    return jnp.asarray(np.block([[real, imag], [-imag, real]]).astype(np.float32), BF16)


def twiddle(first, second, sign, scale=1.0):
    grid = np.outer(np.arange(first), np.arange(second)) % (first * second)
    angles = sign * 2.0 * np.pi / (first * second) * grid
    return np.stack([np.cos(angles) * scale, np.sin(angles) * scale]).astype(np.float32)


def dot(a, b):
    return jnp.dot(a, b, preferred_element_type=F32)


def rotated(re, im, cosine, sine):
    return re * cosine - im * sine, re * sine + im * cosine


def pair(re, im, axis):
    return jnp.concatenate([re.astype(BF16), im.astype(BF16)], axis=axis)


def flat_index(naz):
    return lax.axis_index("rg") * naz + lax.axis_index("az")


def coords(flat, naz):
    return (flat // naz, lax.rem(flat, naz))


def greet_all(me, total, naz):
    barrier = pltpu.get_barrier_semaphore()

    def signal(k, carry):
        pl.semaphore_signal(
            barrier, inc=1, device_id=coords(lax.rem(me + k, total), naz), device_id_type=MESH
        )
        return carry

    lax.fori_loop(1, total, signal, 0)
    pl.semaphore_wait(barrier, total - 1)


def range_chain(re, im, fl, fr, gr, gl, wf, wb, middle):
    spec = dot(fl[...], pair(re, im, 0))
    re, im = rotated(spec[:RA], spec[RA:], wf[0], wf[1])
    spec = dot(pair(re, im, 1), fr[...])
    re, im = middle(spec[:, :RB], spec[:, RB:])
    spec = dot(pair(re, im, 1), gr[...])
    re, im = rotated(spec[:, :RB], spec[:, RB:], wb[0], wb[1])
    spec = dot(gl[...], pair(re, im, 0))
    return spec[:RA], spec[RA:]


def image_kernel(
    total, naz, batches, width, groups,
    raw, phase, fl, fr, gr, gl, wf, wb, rate, awf, awb, squares, kernel_row, weights,
    turned, mag, rows_in, edge_az, edge_rg,
    block, work, ready, x, y, size, base, column_out, rows_out,
    load_sem, own_sem, send_sem, recv_sem, x_sem, size_sem, column_sem, rows_sem,
    back_send, back_recv,
):
    me = flat_index(naz)
    mine = batches * ROWS
    wide = width // groups
    pulses = MA * MB
    eager = min(2, groups)

    def load(b, slot):
        return pltpu.make_async_copy(
            raw.at[:, pl.ds(b * ROWS, ROWS), :], block.at[slot], load_sem.at[slot]
        )

    load(0, 0).start()
    greet_all(me, total, naz)

    def over_peers(act):
        def each(k, carry):
            act(k)
            return carry

        lax.fori_loop(1, total, each, 0)

    def send(g, k, start, count):
        peer = lax.rem(me + k, total)
        return pltpu.make_async_remote_copy(
            src_ref=ready.at[:, pl.ds(start, count), pl.ds(peer * width + g * wide, wide)],
            dst_ref=turned.at[:, pl.ds(me * mine + start, count), pl.ds(g * wide, wide)],
            send_sem=send_sem.at[g, k],
            recv_sem=recv_sem.at[g, k],
            device_id=coords(peer, naz),
            device_id_type=MESH,
        )

    def own(b):
        return pltpu.make_async_copy(
            ready.at[:, pl.ds(b * ROWS, ROWS), pl.ds(me * width, width)],
            turned.at[:, pl.ds(me * mine + b * ROWS, ROWS), :],
            own_sem.at[b],
        )

    def middle(re, im):
        return rotated(re, im, phase[0], phase[1])

    for b in range(batches):
        slot = b % 2
        if b + 1 < batches:
            load(b + 1, 1 - slot).start()
        load(b, slot).wait()

        def spread(n1, carry):
            for c in range(2):
                piece = block[slot, c, :, pl.ds(pl.multiple_of(n1 * RB, RB), RB)].astype(F32)
                for h in range(2):
                    work[c, h, pl.ds(n1, ROWS, stride=RA), :] = piece[:, h * LANES:(h + 1) * LANES]
            return carry

        lax.fori_loop(0, RA, spread, 0, unroll=4)

        def one_pulse(p, carry):
            rows = pl.ds(pl.multiple_of(p * RA, RA), RA)
            re = jnp.concatenate([work[0, 0, rows, :], work[0, 1, rows, :]], axis=1)
            im = jnp.concatenate([work[1, 0, rows, :], work[1, 1, rows, :]], axis=1)
            res = range_chain(re, im, fl, fr, gr, gl, wf, wb, middle)
            for c in range(2):
                for h in range(2):
                    work[c, h, rows, :] = res[c][:, h * LANES:(h + 1) * LANES]
            return carry

        lax.fori_loop(0, ROWS, one_pulse, 0, unroll=2)

        def gather(n1, carry):
            for c in range(2):
                piece = jnp.concatenate(
                    [work[c, h, pl.ds(n1, ROWS, stride=RA), :] for h in range(2)], axis=1
                )
                ready[c, pl.ds(b * ROWS, ROWS), pl.ds(pl.multiple_of(n1 * RB, RB), RB)] = (
                    piece.astype(BF16)
                )
            return carry

        lax.fori_loop(0, RA, gather, 0, unroll=4)
        for g in range(eager):
            over_peers(lambda k: send(g, k, b * ROWS, ROWS).start())
        own(b).start()

    for g in range(eager, groups):
        over_peers(lambda k: send(g, k, 0, mine).start())
    taps = jnp.broadcast_to(kernel_row[...], (MB, pulses))
    base[...] = pltpu.roll(taps, 0, 1, stride=1, stride_axis=0).astype(BF16)
    for b in range(batches):
        own(b).wait()

    parts = wide // CHUNK
    early = (groups - 1) * wide
    lead = min(2, batches)

    def column_in(j, slot):
        return pltpu.make_async_copy(
            turned.at[:, :, pl.ds(j * CHUNK, CHUNK)], x.at[slot], x_sem.at[slot]
        )

    def size_out(j):
        return pltpu.make_async_copy(
            size.at[pl.ds(0, pulses), :], mag.at[:, pl.ds(j * CHUNK, CHUNK)], size_sem
        )

    def column_back(j):
        return pltpu.make_async_copy(
            column_out, edge_az.at[:, pl.ds(j * CHUNK, CHUNK)], column_sem
        )

    def send_back(k, b, column, columns):
        peer = lax.rem(me + k, total)
        return pltpu.make_async_remote_copy(
            src_ref=mag.at[pl.ds(peer * mine + b * ROWS, ROWS), pl.ds(column, columns)],
            dst_ref=rows_in.at[pl.ds(b * ROWS, ROWS), pl.ds(me * width + column, columns)],
            send_sem=back_send.at[b, k],
            recv_sem=back_recv.at[b, k],
            device_id=coords(peer, naz),
            device_id_type=MESH,
        )

    for g in range(groups):
        over_peers(lambda k: send(g, k, 0, mine).wait_recv())
        column_in(g * parts, 0).start()
        if early and g + 1 == groups:
            for b in range(lead):
                over_peers(lambda k: send_back(k, b, 0, early).start())
        for part in range(parts):
            j = g * parts + part
            slot = part % 2
            column_in(j, slot).wait()
            if part + 1 < parts:
                column_in(j + 1, 1 - slot).start()
            azimuth_forward(x.at[slot], awf, y)
            azimuth_middle(rate[:, j * CHUNK:(j + 1) * CHUNK], fl, gl, awb, squares, y, work)
            azimuth_backward(work, size)
            size_out(j).start()
            if part + 1 == parts:
                size_out(j).wait()
                if g + 1 == groups:
                    for b in range(lead):
                        over_peers(lambda k: send_back(k, b, early, wide).start())
            if j > 0:
                column_back(j - 1).wait()

            def edges(m, carry):
                rows = pl.ds(pl.multiple_of(m * MB, MB), MB)
                column_out[rows, :] = dot(base[...], size[pl.ds(pl.multiple_of(m * MB, MB), pulses), :])
                return carry

            lax.fori_loop(0, MA, edges, 0)
            column_back(j).start()
            if part + 1 < parts:
                size_out(j).wait()
    own_rows = pltpu.make_async_copy(
        mag.at[pl.ds(me * mine, mine), :], rows_in.at[:, pl.ds(me * width, width)], size_sem
    )
    own_rows.start()
    own_rows.wait()
    column_back(groups * parts - 1).wait()

    def turn(re, im):
        return -weights[...] * im, weights[...] * re

    def rows_load(b):
        return pltpu.make_async_copy(
            rows_in.at[pl.ds(b * ROWS, ROWS), :], block.at[0, 0], load_sem.at[0]
        )

    def rows_back(b):
        return pltpu.make_async_copy(rows_out, edge_rg.at[pl.ds(b * ROWS, ROWS), :], rows_sem)

    for b in range(batches):
        over_peers(lambda k: send_back(k, b, 0, width).wait_recv())
        if b + lead < batches:
            over_peers(lambda k: send_back(k, b + lead, 0, width).start())
        rows_load(b).start()
        rows_load(b).wait()

        def spread_rows(n1, carry):
            piece = block[0, 0, :, pl.ds(pl.multiple_of(n1 * RB, RB), RB)].astype(F32)
            for h in range(2):
                work[0, h, pl.ds(n1, ROWS, stride=RA), :] = piece[:, h * LANES:(h + 1) * LANES]
            return carry

        lax.fori_loop(0, RA, spread_rows, 0, unroll=4)

        def one_pair(q, carry):
            both = [pl.ds(pl.multiple_of((q + o) * RA, RA), RA) for o in (0, ROWS // 2)]
            re, im = (jnp.concatenate([work[0, 0, r, :], work[0, 1, r, :]], axis=1) for r in both)
            res = range_chain(re, im, fl, fr, gr, gl, wf, wb, turn)
            for c in range(2):
                for h in range(2):
                    work[0, h, both[c], :] = res[c][:, h * LANES:(h + 1) * LANES]
            return carry

        lax.fori_loop(0, ROWS // 2, one_pair, 0, unroll=2)
        if b > 0:
            rows_back(b - 1).wait()

        def gather_rows(n1, carry):
            piece = jnp.concatenate(
                [work[0, h, pl.ds(n1, ROWS, stride=RA), :] for h in range(2)], axis=1
            )
            rows_out[:, pl.ds(pl.multiple_of(n1 * RB, RB), RB)] = piece
            return carry

        lax.fori_loop(0, RA, gather_rows, 0, unroll=4)
        rows_back(b).start()
    rows_back(batches - 1).wait()

    for g in range(groups):
        over_peers(lambda k: send(g, k, 0, mine).wait_send())
    for b in range(batches):
        over_peers(lambda k: send_back(k, b, 0, width).wait_send())


def butterflies(values, sign):
    if len(values) == 1:
        return values
    half = len(values) // 2
    even = butterflies(values[0::2], sign)
    odd = butterflies(values[1::2], sign)
    first, second = [], []
    for k in range(half):
        re, im = odd[k]
        turn = sign * 2.0 * math.pi * k / len(values)
        cosine, sine = math.cos(turn), math.sin(turn)
        if k == 0:
            pass
        elif 4 * k == len(values):
            re, im = (im, -re) if sign < 0 else (-im, re)
        elif abs(abs(cosine) - abs(sine)) < 1e-9:
            size = abs(cosine)
            a = re if cosine > 0 else -re
            b = im if cosine > 0 else -im
            c = re if sine > 0 else -re
            d = im if sine > 0 else -im
            re, im = (a - d) * size, (c + b) * size
        else:
            re, im = re * cosine - im * sine, re * sine + im * cosine
        first.append((even[k][0] + re, even[k][1] + im))
        second.append((even[k][0] - re, even[k][1] - im))
    return first + second


def sincos_fit():
    grid = np.cos(np.linspace(0.0, np.pi, 4001)) * 0.5
    square = grid * grid
    cosine = np.polynomial.chebyshev.Chebyshev.fit(
        square, np.cos(2 * np.pi * grid), 6, domain=[0, 0.25]
    ).convert(kind=np.polynomial.Polynomial).coef
    ratio = np.where(np.abs(grid) < 1e-9, 2 * np.pi, np.sin(2 * np.pi * grid) / np.where(np.abs(grid) < 1e-9, 1.0, grid))
    sine = np.polynomial.chebyshev.Chebyshev.fit(
        square, ratio, 6, domain=[0, 0.25]
    ).convert(kind=np.polynomial.Polynomial).coef
    return [float(x) for x in cosine], [float(x) for x in sine]


def horner(coefs, x):
    value = coefs[-1] * x + coefs[-2]
    for c in coefs[-3::-1]:
        value = value * x + c
    return value


def tile_at(i):
    t, h = i // 2, lax.rem(i, 2)
    return t * ROWS, pl.ds(pl.multiple_of(h * LANES, LANES), LANES)


def rows_at(start):
    return pl.ds(pl.multiple_of(start, ROWS), ROWS)


def azimuth_forward(x, wf, y):
    def one(i, carry):
        top, lanes = tile_at(i)
        values = [
            tuple(x[c, rows_at(m * MB + top), lanes].astype(F32) for c in range(2))
            for m in range(MA)
        ]
        for f, (re, im) in enumerate(butterflies(values, -1.0)):
            re, im = rotated(re, im, wf[0, f, rows_at(top), :], wf[1, f, rows_at(top), :])
            y[f, rows_at(top), lanes] = re.astype(BF16)
            y[f, rows_at(MB + top), lanes] = im.astype(BF16)
        return carry

    lax.fori_loop(0, 2 * (MB // ROWS), one, 0)


def azimuth_middle(rate, fl, gl, wb, squares, y, z):
    cos_fit, sin_fit = sincos_fit()
    turns = rate * (1.0 / (2.0 * math.pi))

    def one(f, carry):
        spec = dot(fl[...], y[f])
        square = jnp.concatenate([squares[f], squares[f]], axis=1)
        turn = turns * square
        turn = turn - jnp.round(turn)
        power = turn * turn
        re, im = rotated(spec[:MB], spec[MB:], horner(cos_fit, power), horner(sin_fit, power) * turn)
        spec = dot(gl[...], pair(re, im, 0))
        cosine = jnp.concatenate([wb[0, f], wb[0, f]], axis=1)
        sine = jnp.concatenate([wb[1, f], wb[1, f]], axis=1)
        rows = pl.ds(pl.multiple_of(f * MB, MB), MB)
        for c, piece in enumerate(rotated(spec[:MB], spec[MB:], cosine, sine)):
            for h in range(2):
                z[c, h, rows, :] = piece[:, h * LANES:(h + 1) * LANES]
        return carry

    lax.fori_loop(0, MA, one, 0)


def azimuth_backward(z, size):
    for h in range(2):
        def one(t, carry):
            top = t * ROWS
            values = [
                tuple(z[c, h, rows_at(f * MB + top), :] for c in range(2)) for f in range(MA)
            ]
            for m, (re, im) in enumerate(butterflies(values, 1.0)):
                value = jnp.sqrt(re * re + im * im).astype(BF16)
                for copy in range(2):
                    rows = rows_at((copy * MA + m) * MB + top)
                    size[rows, h * LANES:(h + 1) * LANES] = value
            return carry

        lax.fori_loop(0, MB // ROWS, one, 0)


def lane_table(table):
    return jnp.asarray(np.repeat(table[..., None], LANES, axis=-1))


def on_device(total, naz, raw_pulses, range_phase, azimuth_rate, conc_azimuth, conc_range):
    mine, bins = raw_pulses.shape[1], raw_pulses.shape[2]
    width = azimuth_rate.shape[0]
    pulses = conc_azimuth.shape[0]
    batches = mine // ROWS
    vmem = pl.BlockSpec(memory_space=pltpu.VMEM)
    hbm = pl.BlockSpec(memory_space=pl.ANY)
    range_tables = (left_table(RA, -1.0), right_table(RB, -1.0), right_table(RB, 1.0), left_table(RA, 1.0))
    range_twiddles = (jnp.asarray(twiddle(RA, RB, -1.0)), jnp.asarray(twiddle(RA, RB, 1.0)))

    with jax.named_scope("tables"):
        groups = max(1, min(4, width // CHUNK))
        grid = range_phase.reshape(RB, RA).T
        phase = jnp.stack([jnp.cos(grid), jnp.sin(grid)])
        scale = 1.0 / math.sqrt(MA)
        freqs = np.arange(MA)[:, None] + MA * np.arange(MB)[None, :]
        signed = np.where(freqs < pulses // 2, freqs, freqs - pulses) / pulses
        squares = lane_table((signed * signed).astype(np.float32))
        half = pulses // 2
        mixed = conc_azimuth[1:half] + conc_azimuth[:half:-1]
        index = np.arange(1, half)
        sines = np.sin(2.0 * np.pi / pulses * (np.outer(index, index) % pulses)) / pulses
        taps = jnp.sum(jnp.asarray(sines.astype(np.float32)) * mixed[None, :], axis=1)
        zero = jnp.zeros((1,), F32)
        kernel_row = jnp.concatenate([zero, taps, zero, -taps[::-1]]).reshape(1, pulses)
        mirrored = jnp.concatenate([conc_range[:1], conc_range[:0:-1]])
        place = jnp.arange(bins, dtype=jnp.int32)
        signs = jnp.where(place < bins // 2, 1.0, -1.0) * ((place != 0) & (place != bins // 2))
        weights = (0.5 * signs * (conc_range + mirrored)).reshape(RB, RA).T

    with jax.named_scope("image"):
        dma = pltpu.SemaphoreType.DMA
        _, _, _, edge_azimuth, edge_range = pl.pallas_call(
            functools.partial(image_kernel, total, naz, batches, width, groups),
            out_shape=(
                jax.ShapeDtypeStruct((2, pulses, width), BF16),
                jax.ShapeDtypeStruct((pulses, width), BF16),
                jax.ShapeDtypeStruct((mine, bins), BF16),
                jax.ShapeDtypeStruct((pulses, width), F32),
                jax.ShapeDtypeStruct((mine, bins), F32),
            ),
            in_specs=[hbm] + [vmem] * 13,
            out_specs=(hbm,) * 5,
            scratch_shapes=[
                pltpu.VMEM((2, 2, ROWS, bins), BF16),
                pltpu.VMEM((2, 2, ROWS * RA, LANES), F32),
                pltpu.VMEM((2, mine, bins), BF16),
                pltpu.VMEM((2, 2, pulses, CHUNK), BF16),
                pltpu.VMEM((MA, 2 * MB, CHUNK), BF16),
                pltpu.VMEM((2 * pulses, CHUNK), BF16),
                pltpu.VMEM((MB, pulses), BF16),
                pltpu.VMEM((pulses, CHUNK), F32),
                pltpu.VMEM((ROWS, bins), F32),
                dma((2,)), dma((batches,)), dma((groups, total)), dma((groups, total)),
                dma((2,)), dma, dma, dma,
                dma((batches, total)), dma((batches, total)),
            ],
            compiler_params=pltpu.CompilerParams(
                collective_id=0, has_side_effects=True, vmem_limit_bytes=VMEM_LIMIT
            ),
            name="image",
        )(
            raw_pulses, phase, *range_tables, *range_twiddles, azimuth_rate.reshape(1, width),
            lane_table(twiddle(MA, MB, -1.0, scale)), lane_table(twiddle(MA, MB, 1.0, scale)),
            squares, kernel_row, weights,
        )
    return edge_azimuth, edge_range


def solution(mesh):
    total = mesh.shape["rg"] * mesh.shape["az"]
    in_specs = (P(None, ("rg", "az"), None), P(), P(("rg", "az")), P(), P())
    out_specs = (P(None, ("rg", "az")), P(("rg", "az"), None))
    return jax.shard_map(
        functools.partial(on_device, total, mesh.shape["az"]),
        mesh=mesh, in_specs=in_specs, out_specs=out_specs, check_vma=False,
    )
```
